32 devices in a mesh: batch: 16 (over z, x, core), head: 2 (over y).
Axes of the slice: x: 2, y: 2, z: 4, core: 2. Of those that a mesh axis runs over, the one named last changes fastest.
Arguments:
- inputs: bfloat16 [32, 16, 44, 256], P(('batch', 'head')), may hold values from -12 to 12
- cot_shared: bfloat16 [32, 8, 22, 512], P(('batch', 'head')), may hold values from -5 to 5
- cot_task: bfloat16 [2, 32, 8, 22, 512], P('head', 'batch'), may hold values from -6 to 6
- trunk_one: float32 [1179648], P(('batch', 'head')), may hold values from -0.125 to 0.125
- trunk_one_first: float32 [1179648], P(('batch', 'head')), may hold values from -20 to 20
- trunk_one_second: float32 [1179648], P(('batch', 'head')), may hold values from 0.90112 to 3.60448
- attention: float32 [2, 524288], P('head', 'batch'), may hold values from -0.25 to 0.25
- attention_first: float32 [2, 524288], P('head', 'batch'), may hold values from -4 to 4
- attention_second: float32 [2, 524288], P('head', 'batch'), may hold values from 0.00518144 to 0.0202752
- head_conv: float32 [2, 2359296], P('head', 'batch'), may hold values from -0.09375 to 0.09375
- head_conv_first: float32 [2, 2359296], P('head', 'batch'), may hold values from -4 to 4
- head_conv_second: float32 [2, 2359296], P('head', 'batch'), may hold values from 0.0946176 to 0.382976
- norm_params: float32 [2, 512], replicated, may hold values from -0.6 to 1.5
- norm_first: float32 [2, 512], replicated, may hold values from -2048 to 2048
- norm_second: float32 [2, 512], replicated, may hold values from 5075.108 to 81201.73
Outputs:
- shared_out: float32 [32, 8, 22, 512], P(('batch', 'head'))
- task_out: float32 [2, 32, 8, 22, 512], P('head', 'batch')
- input_grad: float32 [32, 16, 44, 256], P(('batch', 'head'))
- trunk_one_next: float32 [1179648], P(('batch', 'head'))
- trunk_one_first_next: float32 [1179648], P(('batch', 'head'))
- trunk_one_second_next: float32 [1179648], P(('batch', 'head'))
- attention_next: float32 [2, 524288], P('head', 'batch')
- attention_first_next: float32 [2, 524288], P('head', 'batch')
- attention_second_next: float32 [2, 524288], P('head', 'batch')
- head_conv_next: float32 [2, 2359296], P('head', 'batch')
- head_conv_first_next: float32 [2, 2359296], P('head', 'batch')
- head_conv_second_next: float32 [2, 2359296], P('head', 'batch')
- norm_next: float32 [2, 512], replicated
- norm_first_next: float32 [2, 512], replicated
- norm_second_next: float32 [2, 512], replicated
The draws below stay inside these ranges and needn't reach their ends.
All inputs are finite; a program needn't handle non-finite values.
Results may differ from the reference program's by a relative error of at most 0.0068.
Values may be sent and summed in bfloat16 or wider, within the bound.
No kernel may reach another device: no remote copies, remote signals or barrier semaphores. Data moves between devices by JAX's collectives and lax.ppermute only.
A program may use at most 128 MiB of HBM per device.

```python
import math
import jax
import jax.numpy as jnp
from jax import lax

C_IN = 256
C = 512
H = 16
W = 44
STEP = 10
FRAMES = 32
TASKS = 2


def draw_inputs(key, part):
    key = jax.random.fold_in(key, 3)
    pixel_key = jax.random.fold_in(key, 5)
    frame_pos = jnp.arange(FRAMES, dtype=jnp.float32) / max(FRAMES - 1, 1)
    channel_part = jax.random.normal(key, (FRAMES, H, W, C_IN), jnp.float32)
    pixel_part = jax.random.normal(pixel_key, (FRAMES, H, W, 1), jnp.float32)
    noise_field = jnp.clip(0.6 * channel_part + 0.8 * pixel_part, -4.0, 4.0)
    growth = jnp.exp(jnp.log(3.0) * frame_pos)
    return (noise_field * growth[:, None, None, None]).astype(jnp.bfloat16)


def draw_cot_shared(key, part):
    key = jax.random.fold_in(key, 7)
    sign_key = jax.random.fold_in(key, 21)
    level_key = jax.random.fold_in(key, 22)
    signs = jnp.where(jax.random.bernoulli(sign_key, 0.5, (C,)), 1.0, -1.0).astype(jnp.float32)
    levels = jnp.exp(jax.random.uniform(level_key, (C,), jnp.float32, jnp.log(0.8), jnp.log(1.6)))
    noise_field = 0.8 * jnp.clip(jax.random.normal(key, (FRAMES, H // 2, W // 2, C), jnp.float32), -4.0, 4.0)
    return (noise_field + signs * levels).astype(jnp.bfloat16)


def draw_norm_params(key, part):
    gain_key = jax.random.fold_in(key, 11)
    offset_key = jax.random.fold_in(key, 12)
    gain_rows = 1.0 + 0.2 * jnp.clip(jax.random.normal(gain_key, (1, C), jnp.float32), -2.5, 2.5)
    offset_rows = 0.3 * jnp.clip(jax.random.normal(offset_key, (1, C), jnp.float32), -2.0, 2.0)
    return jnp.concatenate([gain_rows, offset_rows], axis=0)


def level_of(key, dims, shards, least, top_value):
    def one(axis_at, parts):
        heights = jax.random.uniform(jax.random.fold_in(jax.random.fold_in(key, 6), axis_at), (parts,), jnp.float32, least / len(shards), top_value / len(shards))
        return jnp.repeat(jnp.exp(heights), dims[axis_at] // parts).reshape((-1,) + (1,) * (len(dims) - axis_at - 1))

    loudness = one(*shards[0])
    for cut in shards[1:]:
        loudness = loudness * one(*cut)
    return loudness


def noise(own_key, extent, width, limit, cuts=(), held_as=jnp.bfloat16):
    level = level_of(own_key, extent, cuts, -0.22, 0.18) if cuts else 1.0
    array = jax.random.normal(own_key, extent, jnp.float32) * width * level
    return jnp.minimum(jnp.maximum(array, -limit), limit).astype(held_as)


def setup_inputs(seed: int = 0) -> dict:
    seeds = jax.random.split(jax.random.key(seed), 16)
    return {
        "inputs": draw_inputs(jax.random.fold_in(seeds[15], 71), 0),
        "cot_shared": draw_cot_shared(jax.random.fold_in(seeds[15], 71), 0),
        "cot_task": noise(seeds[2], (TASKS, FRAMES, H // 2, W // 2, C), 1.0, 6.0, ((0, 2), (1, 16))),
        "trunk_one": noise(seeds[3], (9 * C_IN * C,), (9 * C_IN) ** -0.5, 0.125, ((0, 32),), jnp.float32),
        "trunk_one_first": noise(seeds[4], (9 * C_IN * C,), (0.022 * (FRAMES * H * W) ** 0.5), 20.0, ((0, 32),), jnp.float32),
        "trunk_one_second": jnp.clip(jnp.exp(math.log(3.60448) - 1.3862944 * jax.random.uniform(seeds[5], (9 * C_IN * C,), jnp.float32) ** level_of(seeds[5], (9 * C_IN * C,), ((0, 32),), -0.2, 0.2)), 0.90112, 3.60448),
        "attention": noise(seeds[6], (TASKS, 2 * C * C), C ** -0.5, 0.25, ((0, 2), (1, 16)), jnp.float32),
        "attention_first": noise(seeds[7], (TASKS, 2 * C * C), (0.0017 * (FRAMES * H * W) ** 0.5), 4.0, ((0, 2), (1, 16)), jnp.float32),
        "attention_second": jnp.clip(jnp.exp(math.log(0.0202752) - 1.3643154 * jax.random.uniform(seeds[8], (TASKS, 2 * C * C), jnp.float32) ** level_of(seeds[8], (TASKS, 2 * C * C), ((0, 2), (1, 16)), -0.2, 0.2)), 0.00518144, 0.0202752),
        "head_conv": noise(seeds[9], (TASKS, 9 * C * C), (9 * C) ** -0.5, 0.09375, ((0, 2), (1, 16)), jnp.float32),
        "head_conv_first": noise(seeds[10], (TASKS, 9 * C * C), (0.0072 * (FRAMES * H * W) ** 0.5), 4.0, ((0, 2), (1, 16)), jnp.float32),
        "head_conv_second": jnp.clip(jnp.exp(math.log(0.382976) - 1.39812883 * jax.random.uniform(seeds[11], (TASKS, 9 * C * C), jnp.float32) ** level_of(seeds[11], (TASKS, 9 * C * C), ((0, 2), (1, 16)), -0.2, 0.2)), 0.0946176, 0.382976),
        "norm_params": draw_norm_params(jax.random.fold_in(seeds[15], 71), 0),
        "norm_first": noise(seeds[13], (2, C), (0.017 * FRAMES * H * W), 2048.0, (), jnp.float32),
        "norm_second": jnp.clip(jnp.exp(jax.random.uniform(seeds[14], (2, C), jnp.float32, math.log(5075.108), math.log(81201.73))), 5075.108, 81201.73),
    }


EPS_NORM = 1e-05
BETA_FIRST = 0.9
BETA_SECOND = 0.999
ADAM_EPS = 1e-08
RATE_MATRIX = 0.02
RATE_NORM = 0.4
WEIGHT_DECAY = 0.01
HIGHEST = lax.Precision.HIGHEST

@jax.custom_vjp
def low(v):
    return lax.optimization_barrier(v.astype(jnp.bfloat16)).astype(jnp.float32)

@jax.custom_vjp
def low_back(v):
    return v

def low_keep(v):
    return (low(v), None)

def low_pass(kept, grad):
    return (grad,)

def back_keep(v):
    return (v, None)

def back_low(kept, grad):
    return (low(grad),)
low.defvjp(low_keep, low_pass)
low_back.defvjp(back_keep, back_low)

def conv_same(field, kernel):
    padded = jnp.pad(field, ((0, 0), (1, 1), (1, 1), (0, 0)))
    height = field.shape[1]
    breadth = field.shape[2]
    summed = jnp.zeros(field.shape[:3] + (kernel.shape[2],), jnp.float32)
    for tap_index in range(9):
        tap_down = tap_index // 3
        tap_across = tap_index % 3
        window = padded[:, tap_down:tap_down + height, tap_across:tap_across + breadth, :]
        summed = summed + jnp.einsum('fhwc,cd->fhwd', window, kernel[tap_index], precision=HIGHEST)
    return summed

def batch_norm(values, gain_row, offset_row):
    center = lax.optimization_barrier(jnp.mean(values, axis=(0, 1, 2)))
    spread = lax.optimization_barrier(jnp.mean(values * values, axis=(0, 1, 2))) - center * center
    return gain_row * (values - center) * lax.rsqrt(spread + EPS_NORM) + offset_row

def mean_pool(values):
    frames, height, breadth, channels = values.shape
    return lax.optimization_barrier(jnp.mean(values.reshape(frames, height // 2, 2, breadth // 2, 2, channels), axis=(2, 4)))

def forward(inputs, kernel_one, attention, head_kernel, norm_params):
    section = low(jax.nn.gelu(batch_norm(low_back(conv_same(inputs, low(kernel_one))), norm_params[0], norm_params[1])))
    shared_out = mean_pool(section)
    results = []
    for task_index in range(attention.shape[0]):
        inner_field = low_back(jnp.einsum('fhwc,cd->fhwd', section, low(attention[task_index, 0]), precision=HIGHEST))
        activated = low(jax.nn.gelu(inner_field))
        logits = low_back(jnp.einsum('fhwc,cd->fhwd', activated, low(attention[task_index, 1]), precision=HIGHEST))
        masked = low(jax.nn.sigmoid(logits) * section)
        head_field = low_back(conv_same(masked, low(head_kernel[task_index])))
        results.append(mean_pool(jax.nn.gelu(head_field)))
    return (shared_out, jnp.stack(results))

def adamw(weight, first_state, second_state, gradient, step_rate):
    first_next = BETA_FIRST * first_state + (1.0 - BETA_FIRST) * gradient
    second_next = BETA_SECOND * second_state + (1.0 - BETA_SECOND) * gradient * gradient
    first_fix = 1.0 - BETA_FIRST ** STEP
    second_fix = 1.0 - BETA_SECOND ** STEP
    update = first_next / first_fix / (jnp.sqrt(second_next / second_fix) + ADAM_EPS)
    return (weight - step_rate * (update + WEIGHT_DECAY * weight), first_next, second_next)

def reference(inputs, cot_shared, cot_task, trunk_one, trunk_one_first, trunk_one_second, attention, attention_first, attention_second, head_conv, head_conv_first, head_conv_second, norm_params, norm_first, norm_second):
    outputs, pullback = jax.vjp(forward, inputs.astype(jnp.float32), trunk_one.reshape(9, C_IN, C), attention.reshape(TASKS, 2, C, C), head_conv.reshape(TASKS, 9, C, C), norm_params)
    gradients = pullback((cot_shared.astype(jnp.float32), cot_task.astype(jnp.float32)))
    input_grad = gradients[0]
    one_new = adamw(trunk_one, trunk_one_first, trunk_one_second, gradients[1].reshape(-1), RATE_MATRIX)
    att_new = adamw(attention, attention_first, attention_second, gradients[2].reshape(TASKS, -1), RATE_MATRIX)
    head_new = adamw(head_conv, head_conv_first, head_conv_second, gradients[3].reshape(TASKS, -1), RATE_MATRIX)
    norm_new = adamw(norm_params, norm_first, norm_second, gradients[4], RATE_NORM)
    return (outputs[0], outputs[1], input_grad, one_new[0], one_new[1], one_new[2], att_new[0], att_new[1], att_new[2], head_new[0], head_new[1], head_new[2], norm_new[0], norm_new[1], norm_new[2])
```

```python
import jax
import jax.numpy as jnp
from jax import lax
from jax.sharding import PartitionSpec as P

STEP = 10


EPS_NORM = 1e-05
BETA_FIRST = 0.9
BETA_SECOND = 0.999
ADAM_EPS = 1e-08
RATE_MATRIX = 0.02
RATE_NORM = 0.4
WEIGHT_DECAY = 0.01


def pad_field(field):
    return jnp.pad(field, ((0, 0), (1, 1), (1, 1), (0, 0)))


def conv_apply(field_low, kernel_low):
    padded = pad_field(field_low)
    height = field_low.shape[1]
    breadth = field_low.shape[2]
    summed = jnp.zeros(field_low.shape[:3] + (kernel_low.shape[2],), jnp.float32)
    for tap_index in range(9):
        tap_down = tap_index // 3
        tap_across = tap_index % 3
        window = padded[:, tap_down : tap_down + height, tap_across : tap_across + breadth, :]
        summed = summed + jnp.einsum(
            "fhwc,cd->fhwd", window, kernel_low[tap_index], preferred_element_type=jnp.float32
        )
    return summed


def conv_input_grad(grad_low, kernel_low):
    padded = pad_field(grad_low)
    height = grad_low.shape[1]
    breadth = grad_low.shape[2]
    summed = jnp.zeros(grad_low.shape[:3] + (kernel_low.shape[1],), jnp.float32)
    for tap_index in range(9):
        tap_down = tap_index // 3
        tap_across = tap_index % 3
        window = padded[
            :, 2 - tap_down : 2 - tap_down + height, 2 - tap_across : 2 - tap_across + breadth, :
        ]
        summed = summed + jnp.einsum(
            "fhwd,cd->fhwc", window, kernel_low[tap_index], preferred_element_type=jnp.float32
        )
    return summed


def conv_kernel_grad(field_low, grad_low):
    padded = pad_field(field_low)
    height = field_low.shape[1]
    breadth = field_low.shape[2]
    tap_grads = []
    for tap_index in range(9):
        tap_down = tap_index // 3
        tap_across = tap_index % 3
        window = padded[:, tap_down : tap_down + height, tap_across : tap_across + breadth, :]
        tap_grads.append(
            jnp.einsum("fhwc,fhwd->cd", window, grad_low, preferred_element_type=jnp.float32)
        )
    return jnp.stack(tap_grads)


def mean_pool(values):
    frames, height, breadth, channels = values.shape
    return jnp.mean(values.reshape(frames, height // 2, 2, breadth // 2, 2, channels), axis=(2, 4))


def pool_back(gradient):
    frames, half_down, half_across, channels = gradient.shape
    spread = jnp.broadcast_to(
        gradient[:, :, None, :, None, :] * 0.25, (frames, half_down, 2, half_across, 2, channels)
    )
    return spread.reshape(frames, half_down * 2, half_across * 2, channels)


def gelu_back(at_point, gradient):
    return jax.vjp(jax.nn.gelu, at_point)[1](gradient)[0]


def adamw(weight, first_state, second_state, gradient, step_rate):
    first_next = BETA_FIRST * first_state + (1.0 - BETA_FIRST) * gradient
    second_next = BETA_SECOND * second_state + (1.0 - BETA_SECOND) * gradient * gradient
    first_fix = 1.0 - BETA_FIRST**STEP
    second_fix = 1.0 - BETA_SECOND**STEP
    update = first_next / first_fix / (jnp.sqrt(second_next / second_fix) + ADAM_EPS)
    return (weight - step_rate * (update + WEIGHT_DECAY * weight), first_next, second_next)


def swap_batch(values, bit):
    return lax.ppermute(values, "batch", [(at, at ^ bit) for at in range(lax.axis_size("batch"))])


def swap_head(values):
    return lax.ppermute(values, "head", [(0, 1), (1, 0)])


def pair_up(mine, other, side, axis):
    first = jnp.where(side == 0, mine, other)
    second = jnp.where(side == 0, other, mine)
    return jnp.stack([first, second], axis=axis)


def half_of(values, side, axis):
    return lax.dynamic_index_in_dim(values, side, axis, keepdims=False)


def batch_side(bit):
    return (lax.axis_index("batch") // bit) % 2


def far_bits():
    bits = []
    bit = lax.axis_size("batch") // 2
    while bit > 2:
        bits.append(bit)
        bit //= 2
    return bits


def sum_batch(values):
    bit = 1
    while bit < lax.axis_size("batch"):
        values = values + swap_batch(values, bit)
        bit *= 2
    return values


def gather_trunk(rows):
    count, breadth = rows.shape
    side_x, side_c, side_h = batch_side(2), batch_side(1), lax.axis_index("head")
    held = rows[None]
    for bit in far_bits():
        other = swap_batch(held, bit)
        held = pair_up(held, other, batch_side(bit), 1).reshape(-1, count, breadth)
    half = held.shape[0] // 2
    one, two = held[:half], held[half:]
    one_other, two_other = swap_batch(one, 2), swap_head(two)
    one = pair_up(one, one_other, side_x, 1)
    two = pair_up(two, two_other, side_h, 1)
    one_other, two_other = swap_head(one), swap_batch(two, 2)
    one = pair_up(one, one_other, side_h, 2)
    two = pair_up(two, two_other, side_x, 1)
    held = jnp.concatenate([one, two], axis=0)
    held = pair_up(held, swap_batch(held, 1), side_c, 2)
    return held.reshape(-1, breadth)


def scatter_trunk(values):
    breadth = values.shape[1]
    groups = lax.axis_size("batch") // 4
    side_x, side_c, side_h = batch_side(2), batch_side(1), lax.axis_index("head")
    held = values.reshape(groups, 2, 2, 2, -1, breadth)

    def give(held, side, axis, swap):
        sent = half_of(held, 1 - side, axis).astype(jnp.bfloat16)
        return half_of(held, side, axis) + swap(sent).astype(jnp.float32)

    held = give(held, side_c, 2, lambda v: swap_batch(v, 1))
    one, two = held[: groups // 2], held[groups // 2 :]
    one = give(one, side_h, 2, swap_head)
    two = give(two, side_x, 1, lambda v: swap_batch(v, 2))
    one = give(one, side_x, 1, lambda v: swap_batch(v, 2))
    two = give(two, side_h, 1, swap_head)
    held = jnp.concatenate([one, two], axis=0)
    for bit in far_bits()[::-1]:
        held = held.reshape((-1, 2) + held.shape[1:])
        held = give(held, batch_side(bit), 1, lambda v, bit=bit: swap_batch(v, bit))
    return held[0]


def body(
    inputs,
    cot_shared,
    cot_task,
    trunk_one,
    trunk_one_first,
    trunk_one_second,
    attention,
    attention_first,
    attention_second,
    head_conv,
    head_conv_first,
    head_conv_second,
    norm_params,
    norm_first,
    norm_second,
):
    channels_in = inputs.shape[3]
    channels = norm_params.shape[1]
    batch = lax.axis_size("batch")
    side_h = lax.axis_index("head")
    total_count = float(
        inputs.shape[0] * inputs.shape[1] * inputs.shape[2] * batch * lax.axis_size("head")
    )
    att_rows = attention.shape[1] // channels
    head_rows = head_conv.shape[1] // channels
    task_low = jnp.concatenate(
        [
            attention.reshape(att_rows, channels).astype(jnp.bfloat16),
            head_conv.reshape(head_rows, channels).astype(jnp.bfloat16),
        ],
        axis=0,
    )
    task_all = lax.all_gather(task_low, "batch", axis=0, tiled=False)
    kernel_one = gather_trunk(trunk_one.reshape(-1, channels).astype(jnp.bfloat16)).reshape(
        9, channels_in, channels
    )
    pair_inputs = pair_up(inputs[0], swap_head(inputs[0]), side_h, 0)
    field_one = conv_apply(pair_inputs, kernel_one)
    local_sums = jnp.stack(
        [jnp.sum(field_one, axis=(0, 1, 2)), jnp.sum(field_one * field_one, axis=(0, 1, 2))]
    )
    total_sum, total_square = sum_batch(local_sums)
    attention_mat = task_all[:, :att_rows].reshape(2, channels, channels)
    head_mat = task_all[:, att_rows:].reshape(9, channels, channels)
    center = total_sum / total_count
    spread = total_square / total_count - center * center
    inverse = lax.rsqrt(spread + EPS_NORM)
    normed = (field_one - center) * inverse
    pre_act = norm_params[0] * normed + norm_params[1]
    gathered = jax.nn.gelu(pre_act).astype(jnp.bfloat16)
    section = lax.dynamic_slice_in_dim(gathered, side_h, 1, 0)
    normed = lax.dynamic_slice_in_dim(normed, side_h, 1, 0)
    pre_act = lax.dynamic_slice_in_dim(pre_act, side_h, 1, 0)
    shared_out = mean_pool(section.astype(jnp.float32))
    inner_field = jnp.einsum(
        "fhwc,cd->fhwd", gathered, attention_mat[0], preferred_element_type=jnp.float32
    )
    activated = jax.nn.gelu(inner_field).astype(jnp.bfloat16)
    logits = jnp.einsum(
        "fhwc,cd->fhwd", activated, attention_mat[1], preferred_element_type=jnp.float32
    )
    mask_field = jax.nn.sigmoid(logits)
    wide_section = gathered.astype(jnp.float32)
    masked = (mask_field * wide_section).astype(jnp.bfloat16)
    head_field = conv_apply(masked, head_mat)
    task_out = mean_pool(jax.nn.gelu(head_field))
    grad_head = gelu_back(head_field, pool_back(cot_task[0].astype(jnp.float32))).astype(
        jnp.bfloat16
    )
    grad_head_kernel = conv_kernel_grad(masked, grad_head)
    grad_masked = conv_input_grad(grad_head, head_mat)
    grad_logits = (grad_masked * wide_section * mask_field * (1.0 - mask_field)).astype(
        jnp.bfloat16
    )
    grad_second_att = jnp.einsum(
        "fhwc,fhwd->cd", activated, grad_logits, preferred_element_type=jnp.float32
    )
    grad_activated = jnp.einsum(
        "fhwd,cd->fhwc", grad_logits, attention_mat[1], preferred_element_type=jnp.float32
    )
    grad_inner = gelu_back(inner_field, grad_activated).astype(jnp.bfloat16)
    grad_first_att = jnp.einsum(
        "fhwc,fhwd->cd", gathered, grad_inner, preferred_element_type=jnp.float32
    )
    feature_back = (
        jnp.einsum(
            "fhwd,cd->fhwc", grad_inner, attention_mat[0], preferred_element_type=jnp.float32
        )
        + grad_masked * mask_field
    )
    back_other = swap_head(half_of(feature_back, 1 - side_h, 0).astype(jnp.bfloat16))
    back_section = (half_of(feature_back, side_h, 0) + back_other.astype(jnp.float32))[None]
    task_grad = jnp.concatenate(
        [
            jnp.stack([grad_first_att, grad_second_att]).reshape(batch, att_rows, channels),
            grad_head_kernel.reshape(batch, head_rows, channels),
        ],
        axis=1,
    ).astype(jnp.bfloat16)
    task_share = lax.psum_scatter(
        task_grad.reshape(-1, channels), "batch", scatter_dimension=0, tiled=True
    ).astype(jnp.float32)
    att_share = task_share[:att_rows].reshape(1, -1)
    head_share = task_share[att_rows:].reshape(1, -1)
    grad_section = pool_back(cot_shared.astype(jnp.float32)) + back_section
    grad_pre = gelu_back(pre_act, grad_section)
    local_sums = jnp.stack(
        [jnp.sum(grad_pre, axis=(0, 1, 2)), jnp.sum(grad_pre * normed, axis=(0, 1, 2))]
    )
    local_sums = local_sums + swap_head(local_sums)
    plain_sum, cross_sum = sum_batch(local_sums)
    grad_field = (
        norm_params[0]
        * inverse
        * (grad_pre - plain_sum / total_count - normed * cross_sum / total_count)
    ).astype(jnp.bfloat16)
    grad_kernel_one = conv_kernel_grad(inputs, grad_field)
    input_grad = conv_input_grad(grad_field, kernel_one)
    one_share = scatter_trunk(grad_kernel_one.reshape(-1, channels)).reshape(-1)
    norm_grad = jnp.stack([cross_sum, plain_sum])
    one_new = adamw(trunk_one, trunk_one_first, trunk_one_second, one_share, RATE_MATRIX)
    att_new = adamw(attention, attention_first, attention_second, att_share, RATE_MATRIX)
    head_new = adamw(head_conv, head_conv_first, head_conv_second, head_share, RATE_MATRIX)
    norm_new = adamw(norm_params, norm_first, norm_second, norm_grad, RATE_NORM)
    return (
        shared_out,
        task_out[None],
        input_grad,
        one_new[0],
        one_new[1],
        one_new[2],
        att_new[0],
        att_new[1],
        att_new[2],
        head_new[0],
        head_new[1],
        head_new[2],
        norm_new[0],
        norm_new[1],
        norm_new[2],
    )


def solution(mesh):
    in_specs = (
        P(("batch", "head"), None, None, None),
        P(("batch", "head"), None, None, None),
        P("head", "batch", None, None, None),
        P(("batch", "head")),
        P(("batch", "head")),
        P(("batch", "head")),
        P("head", "batch"),
        P("head", "batch"),
        P("head", "batch"),
        P("head", "batch"),
        P("head", "batch"),
        P("head", "batch"),
        P(),
        P(),
        P(),
    )
    out_specs = (
        P(("batch", "head"), None, None, None),
        P("head", "batch", None, None, None),
        P(("batch", "head"), None, None, None),
        P(("batch", "head")),
        P(("batch", "head")),
        P(("batch", "head")),
        P("head", "batch"),
        P("head", "batch"),
        P("head", "batch"),
        P("head", "batch"),
        P("head", "batch"),
        P("head", "batch"),
        P(),
        P(),
        P(),
    )
    return jax.shard_map(body, mesh=mesh, in_specs=in_specs, out_specs=out_specs, check_vma=False)
```

```python
import math

import jax
import jax.numpy as jnp
from jax import lax
from jax.experimental import pallas as pl
from jax.experimental.pallas import tpu as pltpu
from jax.sharding import PartitionSpec as P

STEP = 10


EPS_NORM = 1e-05
BETA_FIRST = 0.9
BETA_SECOND = 0.999
ADAM_EPS = 1e-08
RATE_MATRIX = 0.02
RATE_NORM = 0.4
WEIGHT_DECAY = 0.01
GELU_RATE = math.sqrt(2.0 / math.pi)
LANES = 128
VMEM_LIMIT = 40 * 1024 * 1024


def adamw(weight, first_state, second_state, gradient, step_rate):
    first_next = BETA_FIRST * first_state + (1.0 - BETA_FIRST) * gradient
    second_next = BETA_SECOND * second_state + (1.0 - BETA_SECOND) * gradient * gradient
    first_fix = 1.0 - BETA_FIRST**STEP
    second_fix = 1.0 - BETA_SECOND**STEP
    update = first_next / first_fix / (jnp.sqrt(second_next / second_fix) + ADAM_EPS)
    return (weight - step_rate * (update + WEIGHT_DECAY * weight), first_next, second_next)


def swap_batch(values, bit):
    return lax.ppermute(values, "batch", [(at, at ^ bit) for at in range(lax.axis_size("batch"))])


def swap_head(values):
    return lax.ppermute(values, "head", [(0, 1), (1, 0)])


def pair_up(mine, other, side, axis):
    first = jnp.where(side == 0, mine, other)
    second = jnp.where(side == 0, other, mine)
    return jnp.stack([first, second], axis=axis)


def half_of(values, side, axis):
    return lax.dynamic_index_in_dim(values, side, axis, keepdims=False)


def batch_side(bit):
    return (lax.axis_index("batch") // bit) % 2


def far_bits():
    bits = []
    bit = lax.axis_size("batch") // 2
    while bit > 2:
        bits.append(bit)
        bit //= 2
    return bits


def sum_batch(values):
    bit = 1
    while bit < lax.axis_size("batch"):
        values = values + swap_batch(values, bit)
        bit *= 2
    return values


def gather_trunk(rows):
    count, breadth = rows.shape
    side_x, side_c, side_h = batch_side(2), batch_side(1), lax.axis_index("head")
    held = rows[None]
    for bit in far_bits():
        other = swap_batch(held, bit)
        held = pair_up(held, other, batch_side(bit), 1).reshape(-1, count, breadth)
    half = held.shape[0] // 2
    one, two = held[:half], held[half:]
    one_other, two_other = swap_batch(one, 2), swap_head(two)
    one = pair_up(one, one_other, side_x, 1)
    two = pair_up(two, two_other, side_h, 1)
    one_other, two_other = swap_head(one), swap_batch(two, 2)
    one = pair_up(one, one_other, side_h, 2)
    two = pair_up(two, two_other, side_x, 1)
    held = jnp.concatenate([one, two], axis=0)
    held = pair_up(held, swap_batch(held, 1), side_c, 2)
    return held.reshape(-1, breadth)


def scatter_trunk(values):
    breadth = values.shape[1]
    groups = lax.axis_size("batch") // 4
    side_x, side_c, side_h = batch_side(2), batch_side(1), lax.axis_index("head")
    held = values.reshape(groups, 2, 2, 2, -1, breadth)

    def give(held, side, axis, swap):
        sent = half_of(held, 1 - side, axis).astype(jnp.bfloat16)
        return half_of(held, side, axis) + swap(sent).astype(jnp.float32)

    held = give(held, side_c, 2, lambda v: swap_batch(v, 1))
    one, two = held[: groups // 2], held[groups // 2 :]
    one = give(one, side_h, 2, swap_head)
    two = give(two, side_x, 1, lambda v: swap_batch(v, 2))
    one = give(one, side_x, 1, lambda v: swap_batch(v, 2))
    two = give(two, side_h, 1, swap_head)
    held = jnp.concatenate([one, two], axis=0)
    for bit in far_bits()[::-1]:
        held = held.reshape((-1, 2) + held.shape[1:])
        held = give(held, batch_side(bit), 1, lambda v, bit=bit: swap_batch(v, bit))
    return held[0]


def aligned(start, size):
    return pl.ds(pl.multiple_of(start, 16), size)


def wide_of(breadth):
    return (breadth // 16 + 1) * 16


def mm(left, right):
    return lax.dot_general(left, right, (((1,), (0,)), ((), ())), preferred_element_type=jnp.float32)


def mm_right(left, right):
    return lax.dot_general(left, right, (((1,), (1,)), ((), ())), preferred_element_type=jnp.float32)


def mm_left(left, right):
    return lax.dot_general(left, right, (((0,), (0,)), ((), ())), preferred_element_type=jnp.float32)


def gelu_parts(values):
    square = values * values
    turned = jnp.tanh(GELU_RATE * (values + 0.044715 * values * square))
    return square, turned


def gelu(values):
    _, turned = gelu_parts(values)
    return 0.5 * values * (1.0 + turned)


def gelu_slope(values):
    square, turned = gelu_parts(values)
    inner = GELU_RATE * (1.0 + 3.0 * 0.044715 * square)
    return 0.5 * (1.0 + turned) + 0.5 * values * (1.0 - turned * turned) * inner


def gelu_both(values):
    square, turned = gelu_parts(values)
    inner = GELU_RATE * (1.0 + 3.0 * 0.044715 * square)
    half = 0.5 * (1.0 + turned)
    return values * half, half + 0.5 * values * (1.0 - turned * turned) * inner


def inside(rows, wide, breadth):
    at = lax.broadcasted_iota(jnp.int32, (rows, 1), 0)
    return lax.rem(at, wide) < breadth


def spread_columns(values, low_ref, wide):
    pixels, channels = values.shape
    blank = jnp.zeros((wide, low_ref.shape[1]), low_ref.dtype)
    low_ref[0:wide] = blank
    low_ref[wide + pixels : 2 * wide + pixels] = blank
    low_ref[wide : wide + pixels, 0:channels] = pltpu.roll(values, 1, 0).astype(low_ref.dtype)
    low_ref[wide : wide + pixels, channels : 2 * channels] = values.astype(low_ref.dtype)
    low_ref[wide : wide + pixels, 2 * channels : 3 * channels] = pltpu.roll(
        values, pixels - 1, 0
    ).astype(low_ref.dtype)


def call(kernel, outs, scratch=(), smem=0, flops=0, moved=0):
    def run(*operands):
        whole = pl.BlockSpec(memory_space=pltpu.VMEM)
        single = not isinstance(outs, (tuple, list))
        return pl.pallas_call(
            kernel,
            out_shape=outs,
            in_specs=[
                pl.BlockSpec(memory_space=pltpu.SMEM) if at < smem else whole
                for at in range(len(operands))
            ],
            out_specs=whole if single else tuple(whole for _ in outs),
            scratch_shapes=list(scratch),
            compiler_params=pltpu.CompilerParams(vmem_limit_bytes=VMEM_LIMIT),
            cost_estimate=pl.CostEstimate(flops=flops, bytes_accessed=moved, transcendentals=0),
        )(*operands)

    return run


def shape_of(*dims, dtype=jnp.float32):
    return jax.ShapeDtypeStruct(dims, dtype)


def pack_rows(channels, *flat):
    parts = channels // LANES

    def kernel(*refs):
        count = len(refs) // 2
        for source, target in zip(refs[:count], refs[count:]):
            rows = target.shape[0]
            for part in range(parts):
                target[:, part * LANES : (part + 1) * LANES] = source[
                    pl.ds(part, rows, stride=parts), :
                ].astype(jnp.bfloat16)

    sources = [v.reshape(-1, LANES) for v in flat]
    outs = tuple(shape_of(v.size // channels, channels, dtype=jnp.bfloat16) for v in flat)
    return call(kernel, outs, moved=6 * sum(v.size for v in flat))(*sources)


def trunk_forward(mine, other, kernel_rows):
    height, breadth, channels_in = mine.shape
    channels = kernel_rows.shape[1]
    wide = wide_of(breadth)
    pixels = height * wide
    depth = 3 * channels_in
    tile = pixels // 2

    def kernel(mine_ref, other_ref, kernel_ref, field_ref, sums_ref, flat_ref, low_ref):
        flat_ref[...] = jnp.zeros_like(flat_ref)
        total = jnp.zeros((1, channels), jnp.float32)
        square = jnp.zeros((1, channels), jnp.float32)
        for frame, source in enumerate((mine_ref, other_ref)):
            for row in range(height):
                flat_ref[row * wide : row * wide + breadth, :] = source[row].astype(jnp.float32)
            spread_columns(flat_ref[...], low_ref.at[frame], wide)
            for part in range(2):
                start = part * tile
                value = mm(low_ref[frame, start : start + tile, :], kernel_ref[0:depth])
                for step in (1, 2):
                    at = start + step * wide
                    value += mm(
                        low_ref[frame, at : at + tile, :],
                        kernel_ref[step * depth : (step + 1) * depth],
                    )
                value = jnp.where(inside(tile, wide, breadth), value, 0.0)
                field_ref[frame, start : start + tile, :] = value
                total += jnp.sum(value, axis=0, keepdims=True)
                square += jnp.sum(value * value, axis=0, keepdims=True)
        sums_ref[0:1] = total
        sums_ref[1:2] = square

    return call(
        kernel,
        (shape_of(2, pixels, channels), shape_of(2, channels)),
        [
            pltpu.VMEM((pixels, channels_in), jnp.float32),
            pltpu.VMEM((2, pixels + 2 * wide, depth), jnp.bfloat16),
        ],
        flops=2 * 2 * pixels * 3 * depth * channels,
        moved=kernel_rows.size * 2 + 2 * pixels * channels * 4,
    )(mine, other, kernel_rows)


def norm_rows(stats, params, count):
    center = stats[0:1] / count
    spread = stats[1:2] / count - center * center
    inverse = lax.rsqrt(spread + EPS_NORM)
    return center, inverse


def attend(field, stats, params, att_source, height, breadth, count):
    _, pixels, channels = field.shape
    wide = pixels // height
    tile = pixels // 2
    rows = height // 2
    source, att_first, att_rows = att_source
    blocks = source.shape[0]

    def kernel(
        field_ref, stats_ref, params_ref, task_ref,
        section_ref, shared_ref, inner_ref, active_ref, mask_ref, masked_ref,
        att_ref, pool_ref, sem,
    ):
        copies = load_task(task_ref, att_ref, sem, att_first, att_rows)
        for copy in copies:
            copy.start()
        center, inverse = norm_rows(stats_ref[...], params_ref[...], count)
        scale = params_ref[0:1] * inverse
        valid = inside(tile, wide, breadth)
        for frame in range(2):
            for part in range(2):
                at = slice(part * tile, (part + 1) * tile)
                pre = params_ref[0:1] * ((field_ref[frame, at, :] - center) * inverse) + params_ref[1:2]
                low = jnp.where(valid, gelu(pre), 0.0).astype(jnp.bfloat16)
                section_ref[frame, at, :] = low
                if frame == 0:
                    put_parts(pool_ref, low.astype(jnp.float32))
                    pooled = pool_tile(pool_ref, wide)
                    first = part * rows // 2
                    shared_ref[first : first + rows // 2] = pooled[:, : breadth // 2, :]
        for copy in copies:
            copy.wait()
        for frame in range(2):
            for part in range(2):
                at = slice(part * tile, (part + 1) * tile)
                low = section_ref[frame, at, :]
                inner = mm(low, att_ref[0:channels])
                inner_ref[frame, at, :] = inner
                active = gelu(inner).astype(jnp.bfloat16)
                active_ref[frame, at, :] = active
                logits = mm(active, att_ref[channels : 2 * channels])
                mask = 1.0 / (1.0 + jnp.exp(-logits))
                mask_ref[frame, at, :] = mask
                masked_ref[frame, at, :] = (mask * low.astype(jnp.float32)).astype(jnp.bfloat16)

    low_shape = shape_of(2, pixels, channels, dtype=jnp.bfloat16)
    whole = pl.BlockSpec(memory_space=pltpu.VMEM)
    return pl.pallas_call(
        kernel,
        out_shape=(
            low_shape,
            shape_of(rows, breadth // 2, channels),
            shape_of(2, pixels, channels),
            low_shape,
            shape_of(2, pixels, channels),
            low_shape,
        ),
        in_specs=[whole, whole, whole, pl.BlockSpec(memory_space=pl.ANY)],
        out_specs=(whole,) * 6,
        scratch_shapes=[
            pltpu.VMEM((2 * channels, channels), jnp.bfloat16),
            lane_parts(tile, channels),
            pltpu.SemaphoreType.DMA((blocks,)),
        ],
        compiler_params=pltpu.CompilerParams(vmem_limit_bytes=VMEM_LIMIT),
        cost_estimate=pl.CostEstimate(
            flops=2 * 2 * 2 * pixels * channels * channels,
            bytes_accessed=2 * pixels * channels * 18,
            transcendentals=0,
        ),
    )(field, stats, params, source)


def lane_parts(rows, channels):
    return pltpu.VMEM((channels // LANES, rows, LANES), jnp.float32)


def put_parts(parts_ref, values):
    for part in range(parts_ref.shape[0]):
        parts_ref[part] = values[:, part * LANES : (part + 1) * LANES]


def get_parts(parts_ref):
    return jnp.concatenate([parts_ref[part] for part in range(parts_ref.shape[0])], axis=1)


def pool_tile(parts_ref, wide):
    parts, rows, _ = parts_ref.shape
    across = jnp.concatenate(
        [
            parts_ref[part, pl.ds(0, rows // 2, stride=2), :]
            + parts_ref[part, pl.ds(1, rows // 2, stride=2), :]
            for part in range(parts)
        ],
        axis=1,
    )
    down = across.reshape(rows // wide // 2, 2, wide // 2, parts * LANES)
    return (down[:, 0] + down[:, 1]) * 0.25


def lift_tile(values, parts_ref, wide):
    rows, half, channels = values.shape
    values = values * 0.25
    down = jnp.stack([values, values], axis=1).reshape(rows * 2 * half, channels)
    for part in range(parts_ref.shape[0]):
        piece = down[:, part * LANES : (part + 1) * LANES]
        parts_ref[part, pl.ds(0, rows * 2 * half, stride=2), :] = piece
        parts_ref[part, pl.ds(1, rows * 2 * half, stride=2), :] = piece
    return get_parts(parts_ref)


def load_task(task_ref, head_ref, sem, first, rows):
    return [
        pltpu.make_async_copy(
            task_ref.at[block, first : first + rows], head_ref.at[block * rows : (block + 1) * rows], sem.at[block]
        )
        for block in range(task_ref.shape[0])
    ]


def head_forward(side, masked, cot, head_source, height, breadth):
    _, pixels, channels = masked.shape
    wide = pixels // height
    tile = pixels // 2
    rows = height // 2
    source, head_first, head_rows = head_source
    blocks = source.shape[0]
    depth = 3 * channels

    def kernel(
        side_ref, masked_ref, cot_ref, task_ref, out_ref, grad_ref, head_ref, low_ref, pool_ref, lift_ref, cot_wide_ref, sem
    ):
        copies = load_task(task_ref, head_ref, sem, head_first, head_rows)
        for copy in copies:
            copy.start()
        cot_wide_ref[...] = jnp.zeros_like(cot_wide_ref)
        for frame in range(2):
            spread_columns(masked_ref[frame].astype(jnp.float32), low_ref.at[frame], wide)
        for copy in copies:
            copy.wait()
        for frame in range(2):
            own = side_ref[0] if frame == 0 else 1 - side_ref[0]
            for part in range(2):
                start = part * tile
                value = mm(low_ref[frame, start : start + tile, :], head_ref[0:depth])
                for step in (1, 2):
                    at = start + step * wide
                    value += mm(
                        low_ref[frame, at : at + tile, :], head_ref[step * depth : (step + 1) * depth]
                    )
                held, slope = gelu_both(value)
                put_parts(pool_ref, held)
                pooled = pool_tile(pool_ref, wide)
                first = part * rows // 2
                out_ref[own, first : first + rows // 2] = pooled[:, : breadth // 2, :]
                cot_wide_ref[:, : breadth // 2, :] = cot_ref[own, first : first + rows // 2].astype(jnp.float32)
                lifted = lift_tile(cot_wide_ref[...], lift_ref, wide)
                grad_ref[frame, start : start + tile, :] = (slope * lifted).astype(jnp.bfloat16)

    whole = pl.BlockSpec(memory_space=pltpu.VMEM)
    return pl.pallas_call(
        kernel,
        out_shape=(
            shape_of(2, rows, breadth // 2, channels),
            shape_of(2, pixels, channels, dtype=jnp.bfloat16),
        ),
        in_specs=[pl.BlockSpec(memory_space=pltpu.SMEM), whole, whole, pl.BlockSpec(memory_space=pl.ANY)],
        out_specs=(whole, whole),
        scratch_shapes=[
            pltpu.VMEM((blocks * head_rows, channels), jnp.bfloat16),
            pltpu.VMEM((2, pixels + 2 * wide, depth), jnp.bfloat16),
            lane_parts(tile, channels),
            lane_parts(tile, channels),
            pltpu.VMEM((rows // 2, wide // 2, channels), jnp.float32),
            pltpu.SemaphoreType.DMA((blocks,)),
        ],
        compiler_params=pltpu.CompilerParams(vmem_limit_bytes=VMEM_LIMIT),
        cost_estimate=pl.CostEstimate(
            flops=2 * 2 * pixels * 9 * channels * channels,
            bytes_accessed=9 * channels * channels * 2,
            transcendentals=0,
        ),
    )(side, masked, cot, source)


def head_backward(frame, grad, section, inner, mask, att_source, head_source, height, out_type):
    _, pixels, channels = grad.shape
    wide = pixels // height
    tile = pixels // 2
    att_array, att_first, att_rows = att_source
    head_array, head_first, head_rows = head_source
    blocks = head_array.shape[0]

    def kernel(
        grad_ref, section_ref, inner_ref, mask_ref, att_in_ref, head_in_ref, logits_ref, inner_grad_ref, back_ref,
        head_ref, att_ref, low_ref, sem, att_sem,
    ):
        copies = load_task(head_in_ref, head_ref, sem, head_first, head_rows)
        copies += load_task(att_in_ref, att_ref, att_sem, att_first, att_rows)
        for copy in copies:
            copy.start()
        spread_columns(grad_ref[0].astype(jnp.float32), low_ref, wide)
        for copy in copies:
            copy.wait()
        for part in range(2):
            start = part * tile
            at = slice(start, start + tile)
            value = jnp.zeros((tile, channels), jnp.float32)
            for tap in range(9):
                down, across = tap // 3, tap % 3
                first = start + (2 - down) * wide
                value += mm_right(
                    low_ref[first : first + tile, (2 - across) * channels : (3 - across) * channels],
                    head_ref[tap * channels : (tap + 1) * channels],
                )
            mask = mask_ref[0, at, :]
            wide_section = section_ref[0, at, :].astype(jnp.float32)
            logits_grad = (value * wide_section * mask * (1.0 - mask)).astype(jnp.bfloat16)
            logits_ref[at, :] = logits_grad
            active_grad = mm_right(logits_grad, att_ref[channels : 2 * channels])
            inner_grad = (gelu_slope(inner_ref[0, at, :]) * active_grad).astype(jnp.bfloat16)
            inner_grad_ref[at, :] = inner_grad
            back_ref[at, :] = (mm_right(inner_grad, att_ref[0:channels]) + value * mask).astype(out_type)

    low_shape = shape_of(pixels, channels, dtype=jnp.bfloat16)
    one = pl.BlockSpec((1, pixels, channels), lambda at: (frame, 0, 0))
    whole = pl.BlockSpec((pixels, channels), lambda at: (0, 0))
    return pl.pallas_call(
        kernel,
        grid=(1,),
        out_shape=(low_shape, low_shape, shape_of(pixels, channels, dtype=out_type)),
        in_specs=[one, one, one, one] + [pl.BlockSpec(memory_space=pl.ANY)] * 2,
        out_specs=(whole, whole, whole),
        scratch_shapes=[
            pltpu.VMEM((blocks * head_rows, channels), jnp.bfloat16),
            pltpu.VMEM((blocks * att_rows, channels), jnp.bfloat16),
            pltpu.VMEM((pixels + 2 * wide, 3 * channels), jnp.bfloat16),
            pltpu.SemaphoreType.DMA((blocks,)),
            pltpu.SemaphoreType.DMA((blocks,)),
        ],
        compiler_params=pltpu.CompilerParams(vmem_limit_bytes=VMEM_LIMIT),
        cost_estimate=pl.CostEstimate(
            flops=2 * pixels * 11 * channels * channels,
            bytes_accessed=11 * channels * channels * 2,
            transcendentals=0,
        ),
    )(grad, section, inner, mask, att_array, head_array)


def task_gradients(masked, grad, section, active, logits_grads, inner_grads, blocks, height):
    _, pixels, channels = masked.shape
    wide = pixels // height
    att_rows = 2 * channels // blocks
    head_rows = 9 * channels // blocks

    def kernel(
        masked_ref, grad_ref, section_ref, active_ref, logits_one_ref, logits_two_ref, inner_one_ref, inner_two_ref,
        out_ref, low_ref, rows_ref,
    ):
        for frame in range(2):
            spread_columns(masked_ref[frame].astype(jnp.float32), low_ref.at[frame], wide)
        for tap in range(9):
            down, across = tap // 3, tap % 3
            value = jnp.zeros((channels, channels), jnp.float32)
            for frame in range(2):
                value += mm_left(
                    low_ref[frame, down * wide : down * wide + pixels, across * channels : (across + 1) * channels],
                    grad_ref[frame],
                )
            rows_ref[tap * channels : (tap + 1) * channels] = value.astype(jnp.bfloat16)
        for block in range(blocks):
            out_ref[block, att_rows:, :] = rows_ref[block * head_rows : (block + 1) * head_rows]
        value = mm_left(section_ref[0], inner_one_ref[...]) + mm_left(section_ref[1], inner_two_ref[...])
        rows_ref[0:channels] = value.astype(jnp.bfloat16)
        value = mm_left(active_ref[0], logits_one_ref[...]) + mm_left(active_ref[1], logits_two_ref[...])
        rows_ref[channels : 2 * channels] = value.astype(jnp.bfloat16)
        for block in range(blocks):
            out_ref[block, :att_rows, :] = rows_ref[block * att_rows : (block + 1) * att_rows]

    return call(
        kernel,
        shape_of(blocks, att_rows + head_rows, channels, dtype=jnp.bfloat16),
        [
            pltpu.VMEM((2, pixels + 2 * wide, 3 * channels), jnp.bfloat16),
            pltpu.VMEM((9 * channels, channels), jnp.bfloat16),
        ],
        flops=2 * 2 * pixels * 11 * channels * channels,
        moved=11 * channels * channels * 2,
    )(masked, grad, section, active, *logits_grads, *inner_grads)


def norm_backward(field, stats, params, back, back_other, cot, height, breadth, count):
    _, pixels, channels = field.shape
    wide = pixels // height
    tile = pixels // 2
    rows = height // 2

    def kernel(field_ref, stats_ref, params_ref, back_ref, other_ref, cot_ref, grad_ref, sums_ref, cot_wide_ref, lift_ref):
        center, inverse = norm_rows(stats_ref[...], params_ref[...], count)
        cot_wide_ref[...] = jnp.zeros_like(cot_wide_ref)
        plain = jnp.zeros((1, channels), jnp.float32)
        cross = jnp.zeros((1, channels), jnp.float32)
        valid = inside(tile, wide, breadth)
        for part in range(2):
            at = slice(part * tile, (part + 1) * tile)
            first = part * rows // 2
            cot_wide_ref[:, : breadth // 2, :] = cot_ref[0, first : first + rows // 2].astype(jnp.float32)
            lifted = lift_tile(cot_wide_ref[...], lift_ref, wide)
            normed = (field_ref[0, at, :] - center) * inverse
            pre = params_ref[0:1] * normed + params_ref[1:2]
            total = lifted + back_ref[at, :] + other_ref[at, :].astype(jnp.float32)
            value = jnp.where(valid, gelu_slope(pre) * total, 0.0)
            grad_ref[at, :] = value
            plain += jnp.sum(value, axis=0, keepdims=True)
            cross += jnp.sum(value * normed, axis=0, keepdims=True)
        sums_ref[0:1] = plain
        sums_ref[1:2] = cross

    frame = pl.BlockSpec((1, pixels, channels), lambda at: (0, 0, 0))
    flat = pl.BlockSpec((pixels, channels), lambda at: (0, 0))
    small = pl.BlockSpec((2, channels), lambda at: (0, 0))
    pooled = pl.BlockSpec((1, rows, breadth // 2, channels), lambda at: (0, 0, 0, 0))
    return pl.pallas_call(
        kernel,
        grid=(1,),
        out_shape=(shape_of(pixels, channels), shape_of(2, channels)),
        in_specs=[frame, small, small, flat, flat, pooled],
        out_specs=(flat, small),
        scratch_shapes=[
            pltpu.VMEM((rows // 2, wide // 2, channels), jnp.float32),
            lane_parts(tile, channels),
        ],
        compiler_params=pltpu.CompilerParams(vmem_limit_bytes=VMEM_LIMIT),
        cost_estimate=pl.CostEstimate(
            flops=20 * pixels * channels, bytes_accessed=12 * pixels * channels, transcendentals=0
        ),
    )(field, stats, params, back, back_other, cot)


def trunk_backward(inputs, field, stats, params, grad, sums, kernel_rows, count):
    height, breadth, channels_in = inputs.shape
    _, pixels, channels = field.shape
    wide = pixels // height
    tile = pixels // 2

    def kernel(
        inputs_ref, field_ref, stats_ref, params_ref, grad_ref, sums_ref, kernel_ref, rows_ref, back_ref,
        flat_ref, source_ref, low_ref, wide_ref,
    ):
        center, inverse = norm_rows(stats_ref[...], params_ref[...], count)
        flat_ref[...] = jnp.zeros_like(flat_ref)
        for row in range(height):
            flat_ref[row * wide : row * wide + breadth, :] = inputs_ref[row].astype(jnp.float32)
        spread_columns(flat_ref[...], source_ref, wide)
        normed = (field_ref[0] - center) * inverse
        value = params_ref[0:1] * inverse * (
            grad_ref[...] - sums_ref[0:1] / count - normed * sums_ref[1:2] / count
        )
        value = jnp.where(inside(pixels, wide, breadth), value, 0.0)
        spread_columns(value, low_ref, wide)
        for tap in range(9):
            down, across = tap // 3, tap % 3
            rows_ref[tap * channels_in : (tap + 1) * channels_in] = mm_left(
                source_ref[down * wide : down * wide + pixels, across * channels_in : (across + 1) * channels_in],
                low_ref[wide : wide + pixels, channels : 2 * channels],
            )
        for part in range(2):
            start = part * tile
            value = jnp.zeros((tile, channels_in), jnp.float32)
            for tap in range(9):
                down, across = tap // 3, tap % 3
                first = start + (2 - down) * wide
                value += mm_right(
                    low_ref[first : first + tile, (2 - across) * channels : (3 - across) * channels],
                    kernel_ref[tap * channels_in : (tap + 1) * channels_in],
                )
            wide_ref[...] = value
            for row in range(height // 2):
                back_ref[part * height // 2 + row] = wide_ref[row * wide : row * wide + breadth, :]

    frame = pl.BlockSpec((1, pixels, channels), lambda at: (0, 0, 0))
    flat = pl.BlockSpec((pixels, channels), lambda at: (0, 0))
    small = pl.BlockSpec((2, channels), lambda at: (0, 0))
    image = pl.BlockSpec((height, breadth, channels_in), lambda at: (0, 0, 0))
    rows = pl.BlockSpec((9 * channels_in, channels), lambda at: (0, 0))
    return pl.pallas_call(
        kernel,
        grid=(1,),
        out_shape=(shape_of(9 * channels_in, channels), shape_of(height, breadth, channels_in)),
        in_specs=[image, frame, small, small, flat, small, rows],
        out_specs=(rows, image),
        scratch_shapes=[
            pltpu.VMEM((pixels, channels_in), jnp.float32),
            pltpu.VMEM((pixels + 2 * wide, 3 * channels_in), jnp.bfloat16),
            pltpu.VMEM((pixels + 2 * wide, 3 * channels), jnp.bfloat16),
            pltpu.VMEM((tile, channels_in), jnp.float32),
        ],
        compiler_params=pltpu.CompilerParams(vmem_limit_bytes=VMEM_LIMIT),
        cost_estimate=pl.CostEstimate(
            flops=2 * 2 * pixels * 9 * channels_in * channels,
            bytes_accessed=9 * channels_in * channels * 6,
            transcendentals=0,
        ),
    )(inputs, field, stats, params, grad, sums, kernel_rows)


def update_weights(channels, shares, *flat):
    parts = channels // LANES
    count = len(flat) // 3
    lengths = [flat[3 * at].size // channels for at in range(count)]

    def kernel(*refs):
        share_refs, refs = refs[:count], refs[count:]
        sources, targets, (turn_ref,) = refs[: 3 * count], refs[3 * count : 6 * count], refs[6 * count :]
        for at in range(count):
            rows, first = lengths[at], shares[at][1]
            gradient = share_refs[at][first : first + rows].astype(jnp.float32)
            for part in range(parts):
                turn_ref[pl.ds(part, rows, stride=parts), :] = gradient[:, part * LANES : (part + 1) * LANES]
            weight, moment, square = (ref[...] for ref in sources[3 * at : 3 * at + 3])
            news = adamw(weight, moment, square, turn_ref[0 : rows * parts], RATE_MATRIX)
            for target, new in zip(targets[3 * at : 3 * at + 3], news):
                target[...] = new

    sources = [v.reshape(-1, LANES) for v in flat]
    outs = tuple(shape_of(*v.shape) for v in sources)
    news = call(
        kernel, outs, [pltpu.VMEM((max(lengths) * parts, LANES), jnp.float32)], moved=8 * sum(v.size for v in flat)
    )(*[share for share, _ in shares], *sources)
    return [new.reshape(v.shape) for new, v in zip(news, flat)]


def body(
    inputs,
    cot_shared,
    cot_task,
    trunk_one,
    trunk_one_first,
    trunk_one_second,
    attention,
    attention_first,
    attention_second,
    head_conv,
    head_conv_first,
    head_conv_second,
    norm_params,
    norm_first,
    norm_second,
):
    _, height, breadth, channels_in = inputs.shape
    channels = norm_params.shape[1]
    batch = lax.axis_size("batch")
    side = lax.axis_index("head")
    count = float(height * breadth * batch * lax.axis_size("head"))
    att_rows = attention.size // channels
    head_rows = head_conv.size // channels
    blocked = att_rows % 16 == 0 and head_rows % 16 == 0
    att_low, head_low, trunk_low = pack_rows(
        channels, attention.reshape(-1), head_conv.reshape(-1), trunk_one
    )
    task_all = lax.all_gather(jnp.concatenate([att_low, head_low], axis=0), "batch", axis=0, tiled=False)
    if blocked:
        att_source = (task_all, 0, att_rows)
        head_source = (task_all, att_rows, head_rows)
    else:
        att_all = task_all[:, :att_rows].reshape(1, -1, channels)
        head_all = task_all[:, att_rows:].reshape(1, -1, channels)
        att_source = (att_all, 0, att_all.shape[1])
        head_source = (head_all, 0, head_all.shape[1])
    kernel_rows = gather_trunk(trunk_low)
    field, sums = trunk_forward(inputs[0], swap_head(inputs[0]), kernel_rows)
    stats = sum_batch(sums)
    section, shared_out, inner, active, mask, masked = attend(
        field, stats, norm_params, att_source, height, breadth, count
    )
    task_out, grad = head_forward(
        side.reshape(1), masked, cot_task[0], head_source, height, breadth
    )
    backs = [
        head_backward(frame, grad, section, inner, mask, att_source, head_source, height, kind)
        for frame, kind in ((1, jnp.bfloat16), (0, jnp.float32))
    ]
    back_other = swap_head(backs[0][2])
    task_grad = task_gradients(
        masked,
        grad,
        section,
        active,
        (backs[1][0], backs[0][0]),
        (backs[1][1], backs[0][1]),
        batch if blocked else 1,
        height,
    )
    if not blocked:
        att_grad = task_grad[0, : 2 * channels].reshape(batch, att_rows, channels)
        head_grad = task_grad[0, 2 * channels :].reshape(batch, head_rows, channels)
        task_grad = jnp.concatenate([att_grad, head_grad], axis=1)
    task_share = lax.psum_scatter(task_grad, "batch", scatter_dimension=0, tiled=False)
    grad_norm, local = norm_backward(
        field, stats, norm_params, backs[1][2], back_other, cot_shared, height, breadth, count
    )
    sums_back = sum_batch(local + swap_head(local))
    trunk_grad, input_grad = trunk_backward(
        inputs[0], field, stats, norm_params, grad_norm, sums_back, kernel_rows, count
    )
    trunk_share = scatter_trunk(trunk_grad)
    one_new = update_weights(
        channels, [(trunk_share, 0)], trunk_one, trunk_one_first, trunk_one_second
    )
    if blocked:
        shares = [(task_share, 0), (task_share, att_rows)]
    else:
        shares = [(task_share[:att_rows], 0), (task_share[att_rows:], 0)]
    task_new = update_weights(
        channels,
        shares,
        attention,
        attention_first,
        attention_second,
        head_conv,
        head_conv_first,
        head_conv_second,
    )
    norm_new = adamw(norm_params, norm_first, norm_second, sums_back[::-1], RATE_NORM)
    return (
        shared_out[None],
        task_out[None],
        input_grad[None],
        *one_new,
        *task_new,
        *norm_new,
    )


def solution(mesh):
    in_specs = (
        P(("batch", "head"), None, None, None),
        P(("batch", "head"), None, None, None),
        P("head", "batch", None, None, None),
        P(("batch", "head")),
        P(("batch", "head")),
        P(("batch", "head")),
        P("head", "batch"),
        P("head", "batch"),
        P("head", "batch"),
        P("head", "batch"),
        P("head", "batch"),
        P("head", "batch"),
        P(),
        P(),
        P(),
    )
    out_specs = (
        P(("batch", "head"), None, None, None),
        P("head", "batch", None, None, None),
        P(("batch", "head"), None, None, None),
        P(("batch", "head")),
        P(("batch", "head")),
        P(("batch", "head")),
        P("head", "batch"),
        P("head", "batch"),
        P("head", "batch"),
        P("head", "batch"),
        P("head", "batch"),
        P("head", "batch"),
        P(),
        P(),
        P(),
    )
    return jax.shard_map(body, mesh=mesh, in_specs=in_specs, out_specs=out_specs, check_vma=False)
```
